1024 devices in a mesh: gx: 8 (over x_lo, core), gy: 128 (over x_hi, z, y).
Axes of the slice: x: 8 (x_hi: 2, x_lo: 4; x = x_hi * 4 + x_lo), y: 8, z: 8, core: 2. Of those that a mesh axis runs over, the one named last changes fastest.
Arguments:
- tokens: bfloat16 [256, 18432], P('gy', 'gx'), may hold values from -6 to 6
- w_query: bfloat16 [18432, 12288], P('gx', 'gy'), may hold values from -0.046875 to 0.046875
- w_gate_up: bfloat16 [18432, 2, 36864], P('gx', None, 'gy'), may hold values from -0.046875 to 0.046875
- key_cache: bfloat16 [256, 2048, 256], P('gy', 'gx'), may hold values from -480 to 480
- value_cache: bfloat16 [256, 2048, 256], P('gy', 'gx'), may hold values from -6 to 6
- new_kv: bfloat16 [256, 2, 256], P('gy'), may hold values from -6 to 6
- lengths: int32 [256], P('gy'), may hold values from 256 to 2048, as said below
Outputs:
- hidden: bfloat16 [256, 36864], P('gx', 'gy')
- attended: bfloat16 [256, 12288], P('gy', 'gx')
The draws below stay inside these ranges and needn't reach their ends.
Inputs may be any that keep to these rules, and one draw needn't show every extreme that they name: `lengths`: the number of filled slots of each sequence; some sequence has all 2048 filled.
All inputs are finite; a program needn't handle non-finite values.
Results may differ from the reference program's by a relative error of at most 0.02.
Values may be sent and summed in bfloat16 or wider, within the bound.
No kernel may reach another device: no remote copies, remote signals or barrier semaphores. Data moves between devices by JAX's collectives and lax.ppermute only.
A program may use at most 32 MiB of HBM per device.

```python
import jax
import jax.numpy as jnp
from jax import lax

D = 18432
HEADS = 48
HEAD_DIM = 256
FF = 36864
CACHE_LEN = 2048
BATCH = 256


def draw_key_cache(key, part):
    key = jax.random.fold_in(key, 11)
    base = jax.random.normal(key, (BATCH, CACHE_LEN, HEAD_DIM), jnp.float32)
    base = jnp.clip(base, -6.0, 6.0)
    return base.astype(jnp.bfloat16)


def draw_lengths(key, part):
    key = jax.random.fold_in(key, 23)
    lengths = jax.random.randint(key, (BATCH,), CACHE_LEN // 8, CACHE_LEN + 1)
    where = jax.random.randint(jax.random.fold_in(key, 2), (), 0, BATCH)
    return lengths.at[where].set(CACHE_LEN).astype(jnp.int32)


def shard_levels(stream_key, extent, cuts, least, high):
    level = 1.0
    for axis_at, shards_of in cuts:
        steps = jax.random.uniform(jax.random.fold_in(jax.random.fold_in(stream_key, 6), axis_at), (shards_of,), jnp.float32, least / len(cuts), high / len(cuts))
        level = level * jnp.repeat(jnp.exp(steps), extent[axis_at] // shards_of).reshape((-1,) + (1,) * (len(extent) - 1 - axis_at))
    return level


def scatter_about(rng, extent, deviation, limit, split=(), held_as=jnp.bfloat16):
    loudness = shard_levels(rng, extent, split, -0.22, 0.18) if split else 1.0
    entries = jax.random.normal(rng, extent, jnp.float32) * deviation * loudness
    return jnp.minimum(jnp.maximum(entries, -limit), limit).astype(held_as)


def setup_inputs(seed: int = 0) -> dict:
    key_of = jax.random.split(jax.random.key(seed), 8)
    tokens = scatter_about(key_of[0], (BATCH, D), 1.0, 6.0, ((0, 128), (1, 8)))
    w_query = scatter_about(key_of[1], (D, HEADS * HEAD_DIM), D ** -0.5, 0.046875, ((0, 8), (1, 128)))
    w_gate_up = scatter_about(key_of[2], (D, 2, FF), D ** -0.5, 0.046875, ((0, 8), (2, 128)))
    key_cache = draw_key_cache(jax.random.fold_in(key_of[7], 71), 0)
    value_cache = scatter_about(key_of[4], (BATCH, CACHE_LEN, HEAD_DIM), 1.0, 6.0, ((0, 128), (1, 8)))
    new_kv = scatter_about(key_of[5], (BATCH, 2, HEAD_DIM), 1.0, 6.0, ((0, 128),))
    lengths = draw_lengths(jax.random.fold_in(key_of[7], 71), 0)
    return dict(tokens=tokens, w_query=w_query, w_gate_up=w_gate_up, key_cache=key_cache, value_cache=value_cache, new_kv=new_kv, lengths=lengths)


NEG = -1e30


def one_row(query_row, keys, values, key_new, value_new, length):
    scale = HEAD_DIM ** -0.5
    qf = query_row.astype(jnp.float32)
    scores = jnp.dot(qf, keys.astype(jnp.float32).T) * scale
    valid = jnp.arange(CACHE_LEN, dtype=jnp.int32) < length
    scores = jnp.where(valid[None, :], scores, NEG)
    own = jnp.sum(qf * key_new.astype(jnp.float32)[None, :], axis=1) * scale
    top = jnp.maximum(jnp.max(scores, axis=1), own)
    probs = jnp.where(valid[None, :], jnp.exp(scores - top[:, None]), 0.0)
    own_prob = jnp.exp(own - top)
    total = jnp.sum(probs, axis=1) + own_prob
    mixed = jnp.dot(probs, values.astype(jnp.float32)) + own_prob[:, None] * value_new.astype(jnp.float32)[None, :]
    return (mixed / total[:, None]).reshape(HEADS * HEAD_DIM).astype(jnp.bfloat16)


def reference(tokens, w_query, w_gate_up, key_cache, value_cache, new_kv, lengths):
    query = jnp.dot(tokens, w_query, preferred_element_type=jnp.float32).astype(jnp.bfloat16)
    gate_up = jnp.dot(tokens, w_gate_up.reshape(D, 2 * FF), preferred_element_type=jnp.float32)
    hidden = (jax.nn.silu(gate_up[:, :FF]) * gate_up[:, FF:]).astype(jnp.bfloat16)
    query3 = query.reshape(BATCH, HEADS, HEAD_DIM)

    def step(args):
        return one_row(*args)

    attended = lax.map(step, (query3, key_cache, value_cache, new_kv[:, 0, :], new_kv[:, 1, :], lengths))
    return hidden, attended
```

```python
import jax
import jax.numpy as jnp
from jax import lax
from jax.experimental import pallas as pl
from jax.experimental.pallas import tpu as pltpu
from jax.sharding import Mesh, PartitionSpec as P

NEG = -1e30
GX = ("xl", "core")
GY = ("xh", "z", "y")
ALL = GX + GY
LATTICE = ("xh", "z", "y")
PLANE = ("core", "z", "y")


def far_groups():
    return [
        [xh * 64 + (zh * 2 + zlo) * 8 + yh * 2 + ylo for xh in range(2) for zh in range(4) for yh in range(4)]
        for zlo in range(2)
        for ylo in range(2)
    ]


def near_groups():
    groups = []
    for core in range(2):
        for zb in range(4):
            for yb in range(4):
                zs = sorted(((2 * zb + i + core) % 8 for i in range(2)), key=lambda v: v % 2)
                ys = sorted(((2 * yb + i + core) % 8 for i in range(2)), key=lambda v: v % 2)
                groups.append([core * 64 + z * 8 + y for z in zs for y in ys])
    return groups


def query_groups():
    def half(g, h):
        return [g * 128 + h * 16 + i for i in range(16)]

    pairs = [(g, h) for g in range(8) for h in range(g + 1, 8)]
    return [half(g, h) + half(h, g) for g, h in pairs] + [half(g, g) + half(g + 1, g + 1) for g in range(0, 8, 2)]


def exchange(x, axis, groups=None):
    return lax.all_to_all(x, axis, 0, 0, axis_index_groups=groups, tiled=True)


def spread(x, axis, n, groups=None):
    return exchange(jnp.broadcast_to(x[None], (n,) + x.shape), axis, groups)


def beside(x):
    return lax.ppermute(x, "xl", [(i, i ^ 1) for i in range(4)])


def across(x):
    return lax.ppermute(x, "xl", [(i, i ^ 2) for i in range(4)])


def other_core(x):
    return lax.ppermute(x, "core", [(0, 1), (1, 0)])


NT = (((1,), (1,)), ((), ()))
LIMIT = pltpu.CompilerParams(vmem_limit_bytes=16 * 2**20)


def project_kernel(x_ref, wg_ref, wq_ref, out_ref, acc_ref):
    x = x_ref[...]
    width, qw = wg_ref.shape[0], wq_ref.shape[0]
    gate_up = lax.dot_general(x, wg_ref[...], NT, preferred_element_type=jnp.float32)
    query = lax.dot_general(x, wq_ref[...], NT, preferred_element_type=jnp.float32)
    for p in range(4):
        rows = slice(p * 64, p * 64 + 64)
        acc_ref[:, p * 8 : p * 8 + 8, :width] = gate_up[rows].reshape(8, 8, width)
        part = query[rows].reshape(8, 8, qw)
        acc_ref[:, p * 8 : p * 8 + 8, width : width + qw] = part
        acc_ref[:, p * 8 : p * 8 + 8, width + qw :] = part - part.astype(jnp.bfloat16).astype(jnp.float32)
    out_ref[...] = acc_ref[...].astype(jnp.bfloat16)


def project(rows, w_query, w_gate_up):
    d, _, width = w_gate_up.shape
    wg = w_gate_up.transpose(1, 2, 0).reshape(2 * width, d)
    wq = w_query.T
    shape = (8, rows.shape[0] // 8, 2 * width + 2 * wq.shape[0])
    return pl.pallas_call(
        project_kernel,
        out_shape=jax.ShapeDtypeStruct(shape, jnp.bfloat16),
        scratch_shapes=[pltpu.VMEM(shape, jnp.float32)],
        compiler_params=LIMIT,
    )(rows, wg, wq)


def attend_kernel(order, place_ref, lengths_ref, q_ref, *refs):
    n = len(order)
    keys, values, (mine_ref, theirs_ref) = refs[:n], refs[n : 2 * n], refs[2 * n :]
    seqs, block_len, head_dim = keys[0].shape
    scale = head_dim ** (-0.5)
    slot = lax.broadcasted_iota(jnp.int32, (16, block_len), 1)
    for r in range(seqs):
        q = q_ref[r]
        scores, valid = [], []
        for j, flip in enumerate(order):
            s = lax.dot_general(q, keys[j][r], NT, preferred_element_type=jnp.float32) * scale
            start = jnp.bitwise_xor(place_ref[0], flip) * block_len
            valid.append(slot + start < lengths_ref[r])
            scores.append(jnp.where(valid[j], s, NEG))
        top = scores[0]
        for s in scores[1:]:
            top = jnp.maximum(top, s)
        top = jnp.max(top, axis=1, keepdims=True)
        total = jnp.zeros((16, 1), jnp.float32)
        mixed = jnp.zeros((16, head_dim), jnp.float32)
        for j in range(n):
            p = jnp.where(valid[j], jnp.exp(scores[j] - top), 0.0)
            total += jnp.sum(p, axis=1, keepdims=True)
            mixed += jnp.dot(p.astype(jnp.bfloat16), values[j][r], preferred_element_type=jnp.float32)
        for ref, rows in ((mine_ref, slice(0, 8)), (theirs_ref, slice(8, 16))):
            ref[r, :, :head_dim] = mixed[rows]
            lane = lax.broadcasted_iota(jnp.int32, (8, 128), 1)
            ref[r, :, head_dim:] = jnp.where(lane < 64, top[rows], total[rows])


def attend(place, lengths, queries, keys, values, order):
    seqs, _, head_dim = queries.shape
    smem, vmem = pl.BlockSpec(memory_space=pltpu.SMEM), pl.BlockSpec(memory_space=pltpu.VMEM)
    out = jax.ShapeDtypeStruct((seqs, 8, head_dim + 128), jnp.float32)

    def kernel(*refs):
        attend_kernel(order, *refs)

    return pl.pallas_call(
        kernel,
        in_specs=[smem, smem] + [vmem] * (1 + 2 * len(order)),
        out_specs=(vmem, vmem),
        out_shape=(out, out),
        compiler_params=LIMIT,
    )(place.reshape(1).astype(jnp.int32), lengths, queries, *keys, *values)


def finish_kernel(heads, mine_ref, theirs_ref, q_ref, new_ref, out_ref):
    seqs, _, head_dim = q_ref.shape
    scale = head_dim ** (-0.5)
    results = []
    for r in range(seqs):
        mine, theirs = mine_ref[r], theirs_ref[r]
        new = new_ref[r].astype(jnp.float32)
        q = q_ref[r].astype(jnp.float32)[:8]
        own = jnp.sum(q * new[0:1], axis=1, keepdims=True) * scale
        tops = [p[:, head_dim : head_dim + 1] for p in (mine, theirs)]
        sums = [p[:, head_dim + 64 : head_dim + 65] for p in (mine, theirs)]
        top = jnp.maximum(jnp.maximum(tops[0], tops[1]), own)
        w0, w1, w2 = jnp.exp(tops[0] - top), jnp.exp(tops[1] - top), jnp.exp(own - top)
        numer = mine[:, :head_dim] * w0 + theirs[:, :head_dim] * w1 + w2 * new[1:2]
        results.append(numer / (sums[0] * w0 + sums[1] * w1 + w2))
    for h in range(heads):
        rows = jnp.concatenate([x[h : h + 1] for x in results], axis=0)
        out_ref[:, h * head_dim : (h + 1) * head_dim] = rows.astype(jnp.bfloat16)


def finish(mine, theirs, queries, new_kv, heads):
    def kernel(*refs):
        finish_kernel(heads, *refs)

    seqs, _, head_dim = queries.shape
    return pl.pallas_call(
        kernel,
        out_shape=jax.ShapeDtypeStruct((seqs, heads * head_dim), jnp.bfloat16),
        compiler_params=LIMIT,
    )(mine, theirs, queries, new_kv)


def body(tokens, w_query, w_gate_up, key_cache, value_cache, new_kv, lengths):
    f32, bf16 = jnp.float32, jnp.bfloat16
    d, width, qw = tokens.shape[1], w_gate_up.shape[2], w_query.shape[1]
    seqs, _, head_dim = key_cache.shape

    keys_b = beside(key_cache)
    rows = spread(tokens, LATTICE, 32, far_groups()).reshape(64, d)
    rows, keys_b = lax.optimization_barrier((rows, keys_b))
    values_b, keys_c = beside(value_cache), other_core(key_cache)
    rows = spread(rows, PLANE, 4, near_groups()).reshape(256, d)
    rows, values_b, keys_c = lax.optimization_barrier((rows, values_b, keys_c))
    values_c, keys_d, values_d = other_core(value_cache), other_core(keys_b), other_core(values_b)

    got = exchange(project(rows, w_query, w_gate_up), GX).astype(f32)
    total = jnp.sum(got, axis=0)
    hidden = (jax.nn.silu(total[:, :width]) * total[:, width : 2 * width]).astype(bf16)
    hidden = hidden.reshape(2, 2, 4, 2, width).transpose(0, 2, 1, 3, 4).reshape(32, width)
    query = (total[:, 2 * width : 2 * width + qw] + total[:, 2 * width + qw :]).astype(bf16)

    query = query.reshape(2, 2, 4, 2, qw).transpose(0, 2, 1, 3, 4).reshape(16, 2, qw)
    query = exchange(jnp.concatenate([query, query], axis=0), ALL, query_groups())
    place = lax.axis_index(GX)
    block = lax.axis_index("xh") * 4 + lax.axis_index("z") // 2
    sender = jnp.where(place == block, place % 2, (place < block).astype(place.dtype))
    query = lax.dynamic_slice_in_dim(query, sender * 16, 16, 0)
    per_dev = 16 * qw // head_dim
    query = query.transpose(1, 0, 2).reshape(seqs, per_dev, head_dim)
    query = jnp.pad(query, ((0, 0), (0, 8 - per_dev), (0, 0)))
    queries = jnp.concatenate([query, across(query)], axis=1)

    keys = (key_cache, keys_b, keys_c, keys_d)
    values = (value_cache, values_b, values_c, values_d)
    mine, theirs = attend(place, lengths, queries, keys, values, (0, 2, 1, 3))
    attended = finish(mine, across(theirs), queries, new_kv, per_dev)
    return (hidden, attended)


def solution(mesh):
    fine = Mesh(mesh.devices.reshape(4, 2, 2, 8, 8), GX + GY)
    return jax.shard_map(
        body,
        mesh=fine,
        in_specs=(
            P(GY, GX),
            P(GX, GY),
            P(GX, None, GY),
            P(GY, GX, None),
            P(GY, GX, None),
            P(GY, None, None),
            P(GY),
        ),
        out_specs=(P(GX, GY), P(GY, GX)),
        check_vma=False,
    )
```

```python
import jax
import jax.numpy as jnp
from jax import lax
from jax.experimental import pallas as pl
from jax.experimental.pallas import tpu as pltpu
from jax.sharding import Mesh, PartitionSpec as P

NEG = -1e30
GX = ("xl", "core")
GY = ("xh", "z", "y")
ALL = GX + GY
LATTICE = ("xh", "z", "y")
PLANE = ("core", "z", "y")


def far_groups():
    return [
        [xh * 64 + (zh * 2 + zlo) * 8 + yh * 2 + ylo for xh in range(2) for zh in range(4) for yh in range(4)]
        for zlo in range(2)
        for ylo in range(2)
    ]


def near_groups():
    groups = []
    for core in range(2):
        for zb in range(4):
            for yb in range(4):
                zs = sorted(((2 * zb + i + core) % 8 for i in range(2)), key=lambda v: v % 2)
                ys = sorted(((2 * yb + i + core) % 8 for i in range(2)), key=lambda v: v % 2)
                groups.append([core * 64 + z * 8 + y for z in zs for y in ys])
    return groups


def query_groups():
    def half(g, h, lo):
        return [g * 128 + h * 16 + lo * 8 + y for y in range(8)]

    groups = []
    for lo in range(2):
        groups += [half(g, h, lo) + half(h, g, lo) for g in range(8) for h in range(g + 1, 8)]
        groups += [half(g, g, lo) + half(g + 1, g + 1, lo) for g in range(0, 8, 2)]
    return groups


def column_groups():
    return [
        [(hi * 2 + xlo) * 8 + zh * 2 + zlo for hi in range(2) for zlo in range(2)] for xlo in range(2) for zh in range(4)
    ]


def exchange(x, axis, groups=None):
    return lax.all_to_all(x, axis, 0, 0, axis_index_groups=groups, tiled=True)


def spread(x, axis, n, groups=None):
    return exchange(jnp.broadcast_to(x[None], (n,) + x.shape), axis, groups)


def beside(x):
    return lax.ppermute(x, "xl", [(i, i ^ 1) for i in range(4)])


def across(x):
    return lax.ppermute(x, "xl", [(i, i ^ 2) for i in range(4)])


def other_core(x):
    return lax.ppermute(x, "core", [(0, 1), (1, 0)])


NT = (((1,), (1,)), ((), ()))
LIMIT = pltpu.CompilerParams(vmem_limit_bytes=16 * 2**20)


def project_kernel(qw, x_ref, w_ref, out_ref, acc_ref):
    full = lax.dot_general(x_ref[...], w_ref[...], NT, preferred_element_type=jnp.float32)
    width = full.shape[1]
    query = full[:, width - qw :]
    low = query - query.astype(jnp.bfloat16).astype(jnp.float32)
    for p in range(4):
        rows = slice(p * 64, p * 64 + 64)
        acc_ref[:, p * 8 : p * 8 + 8, :width] = full[rows].reshape(8, 8, width)
        acc_ref[:, p * 8 : p * 8 + 8, width:] = low[rows].reshape(8, 8, qw)
    out_ref[...] = acc_ref[...].astype(jnp.bfloat16)


def project(rows, weights, qw):
    def kernel(*refs):
        project_kernel(qw, *refs)

    shape = (8, rows.shape[0] // 8, weights.shape[0] + qw)
    return pl.pallas_call(
        kernel,
        out_shape=jax.ShapeDtypeStruct(shape, jnp.bfloat16),
        scratch_shapes=[pltpu.VMEM(shape, jnp.float32)],
        compiler_params=LIMIT,
    )(rows, weights)


def attend_kernel(order, place_ref, lengths_ref, q_ref, *refs):
    n = len(order)
    keys, values, (mine_ref, theirs_ref) = refs[:n], refs[n : 2 * n], refs[2 * n :]
    seqs, block_len, head_dim = keys[0].shape
    scale = head_dim ** (-0.5)
    slot = lax.broadcasted_iota(jnp.int32, (16, block_len), 1)
    for r in range(seqs):
        q = q_ref[r]
        scores, valid = [], []
        for j, flip in enumerate(order):
            s = lax.dot_general(q, keys[j][r], NT, preferred_element_type=jnp.float32) * scale
            start = jnp.bitwise_xor(place_ref[0], flip) * block_len
            valid.append(slot + start < lengths_ref[r])
            scores.append(jnp.where(valid[j], s, NEG))
        top = scores[0]
        for s in scores[1:]:
            top = jnp.maximum(top, s)
        top = jnp.max(top, axis=1, keepdims=True)
        total = jnp.zeros((16, 1), jnp.float32)
        mixed = jnp.zeros((16, head_dim), jnp.float32)
        for j in range(n):
            p = jnp.where(valid[j], jnp.exp(scores[j] - top), 0.0)
            total += jnp.sum(p, axis=1, keepdims=True)
            mixed += jnp.dot(p.astype(jnp.bfloat16), values[j][r], preferred_element_type=jnp.float32)
        for ref, rows in ((mine_ref, slice(0, 8)), (theirs_ref, slice(8, 16))):
            ref[r, :, :head_dim] = mixed[rows]
            lane = lax.broadcasted_iota(jnp.int32, (8, 128), 1)
            ref[r, :, head_dim:] = jnp.where(lane < 64, top[rows], total[rows])


def attend(place, lengths, queries, keys, values, order):
    seqs, _, head_dim = queries.shape
    smem, vmem = pl.BlockSpec(memory_space=pltpu.SMEM), pl.BlockSpec(memory_space=pltpu.VMEM)
    out = jax.ShapeDtypeStruct((seqs, 8, head_dim + 128), jnp.float32)

    def kernel(*refs):
        attend_kernel(order, *refs)

    return pl.pallas_call(
        kernel,
        in_specs=[smem, smem] + [vmem] * (1 + 2 * len(order)),
        out_specs=(vmem, vmem),
        out_shape=(out, out),
        compiler_params=LIMIT,
    )(place.reshape(1).astype(jnp.int32), lengths, queries, *keys, *values)


def finish_kernel(heads, mine_ref, theirs_ref, q_ref, new_ref, out_ref):
    seqs, _, head_dim = q_ref.shape
    scale = head_dim ** (-0.5)
    results = []
    for r in range(seqs):
        mine, theirs = mine_ref[r], theirs_ref[r]
        new = new_ref[r].astype(jnp.float32)
        q = q_ref[r].astype(jnp.float32)[:8]
        own = jnp.sum(q * new[0:1], axis=1, keepdims=True) * scale
        tops = [p[:, head_dim : head_dim + 1] for p in (mine, theirs)]
        sums = [p[:, head_dim + 64 : head_dim + 65] for p in (mine, theirs)]
        top = jnp.maximum(jnp.maximum(tops[0], tops[1]), own)
        w0, w1, w2 = jnp.exp(tops[0] - top), jnp.exp(tops[1] - top), jnp.exp(own - top)
        numer = mine[:, :head_dim] * w0 + theirs[:, :head_dim] * w1 + w2 * new[1:2]
        results.append(numer / (sums[0] * w0 + sums[1] * w1 + w2))
    for h in range(heads):
        rows = jnp.concatenate([x[h : h + 1] for x in results], axis=0)
        out_ref[:, h * head_dim : (h + 1) * head_dim] = rows.astype(jnp.bfloat16)


def finish(mine, theirs, queries, new_kv, heads):
    def kernel(*refs):
        finish_kernel(heads, *refs)

    seqs, _, head_dim = queries.shape
    return pl.pallas_call(
        kernel,
        out_shape=jax.ShapeDtypeStruct((seqs, heads * head_dim), jnp.bfloat16),
        compiler_params=LIMIT,
    )(mine, theirs, queries, new_kv)


def body(tokens, w_query, w_gate_up, key_cache, value_cache, new_kv, lengths):
    f32, bf16 = jnp.float32, jnp.bfloat16
    d, width, qw = tokens.shape[1], w_gate_up.shape[2], w_query.shape[1]
    seqs, _, head_dim = key_cache.shape

    keys_b, keys_c = beside(key_cache), other_core(key_cache)
    weights = jnp.concatenate([w_gate_up.transpose(1, 2, 0).reshape(2 * width, d), w_query.T], axis=0)
    rows = spread(tokens, LATTICE, 32, far_groups()).reshape(64, d)
    rows, weights, keys_b, keys_c = lax.optimization_barrier((rows, weights, keys_b, keys_c))
    values_b = beside(value_cache)
    rows = spread(rows, PLANE, 4, near_groups()).reshape(256, d)
    rows, values_b = lax.optimization_barrier((rows, values_b))
    values_c, keys_d, values_d = other_core(value_cache), other_core(keys_b), other_core(values_b)

    got = exchange(project(rows, weights, qw), GX).astype(f32)
    total = jnp.sum(got, axis=0)
    hidden = (jax.nn.silu(total[:, :width]) * total[:, width : 2 * width]).astype(bf16)
    hidden = hidden.reshape(2, 2, 4, 2, width).transpose(0, 2, 1, 3, 4).reshape(32, width)
    query = (total[:, 2 * width : 2 * width + qw] + total[:, 2 * width + qw :]).astype(bf16)

    query = query.reshape(2, 2, 4, 2, qw).transpose(2, 1, 0, 3, 4).reshape(8, 4, qw)
    query = exchange(jnp.concatenate([query, query], axis=0), ALL, query_groups())
    place = lax.axis_index(GX)
    block = lax.axis_index("xh") * 4 + lax.axis_index("z") // 2
    sender = jnp.where(place == block, place % 2, (place < block).astype(place.dtype))
    query = lax.dynamic_slice_in_dim(query, sender * 8, 8, 0)
    query = query.reshape(8, 2, seqs, qw).transpose(1, 2, 0, 3).reshape(2, seqs, 8 * qw)
    query = jnp.concatenate([query, query], axis=0)
    query = exchange(query, ("xl", "z"), column_groups())
    per_dev = 16 * qw // head_dim
    query = query.reshape(2, 2, seqs, 8 * qw).transpose(0, 2, 1, 3).reshape(2, seqs, per_dev, head_dim)
    query = jnp.pad(query, ((0, 0), (0, 0), (0, 8 - per_dev), (0, 0)))
    upper = lax.axis_index("xl") >= 2
    own, other = jnp.where(upper, query[1], query[0]), jnp.where(upper, query[0], query[1])
    queries = jnp.concatenate([own, other], axis=1)

    keys = (key_cache, keys_b, keys_c, keys_d)
    values = (value_cache, values_b, values_c, values_d)
    mine, theirs = attend(place, lengths, queries, keys, values, (0, 2, 1, 3))
    attended = finish(mine, across(theirs), queries, new_kv, per_dev)
    return (hidden, attended)


def solution(mesh):
    fine = Mesh(mesh.devices.reshape(4, 2, 2, 8, 8), GX + GY)
    return jax.shard_map(
        body,
        mesh=fine,
        in_specs=(
            P(GY, GX),
            P(GX, GY),
            P(GX, None, GY),
            P(GY, GX, None),
            P(GY, GX, None),
            P(GY, None, None),
            P(GY),
        ),
        out_specs=(P(GX, GY), P(GY, GX)),
        check_vma=False,
    )
```

```python
import jax
import jax.numpy as jnp
from jax import lax
from jax.experimental import pallas as pl
from jax.experimental.pallas import tpu as pltpu
from jax.sharding import Mesh, PartitionSpec as P

NEG = -1e30
GX = ("xl", "core")
GY = ("xh", "z", "y")
ALL = GX + GY
LATTICE = ("xh", "z", "y")
PLANE = ("core", "z", "y")


def far_groups():
    return [
        [xh * 64 + (zh * 2 + zlo) * 8 + yh * 2 + ylo for xh in range(2) for zh in range(4) for yh in range(4)]
        for zlo in range(2)
        for ylo in range(2)
    ]


def near_groups():
    groups = []
    for core in range(2):
        for zb in range(4):
            for yb in range(4):
                zs = sorted(((2 * zb + i + core) % 8 for i in range(2)), key=lambda v: v % 2)
                ys = sorted(((2 * yb + i + core) % 8 for i in range(2)), key=lambda v: v % 2)
                groups.append([core * 64 + z * 8 + y for z in zs for y in ys])
    return groups


def query_groups():
    def half(g, h, lo):
        return [g * 128 + h * 16 + lo * 8 + y for y in range(8)]

    groups = []
    for lo in range(2):
        groups += [half(g, h, lo) + half(h, g, lo) for g in range(8) for h in range(g + 1, 8)]
        groups += [half(g, g, lo) + half(g + 1, g + 1, lo) for g in range(0, 8, 2)]
    return groups


def column_groups():
    return [
        [(hi * 2 + xlo) * 8 + zh * 2 + zlo for hi in range(2) for zlo in range(2)] for xlo in range(2) for zh in range(4)
    ]


def exchange(x, axis, groups=None):
    return lax.all_to_all(x, axis, 0, 0, axis_index_groups=groups, tiled=True)


def spread(x, axis, n, groups=None):
    return exchange(jnp.broadcast_to(x[None], (n,) + x.shape), axis, groups)


def beside(x):
    return lax.ppermute(x, "xl", [(i, i ^ 1) for i in range(4)])


def across(x):
    return lax.ppermute(x, "xl", [(i, i ^ 2) for i in range(4)])


def other_core(x):
    return lax.ppermute(x, "core", [(0, 1), (1, 0)])


NT = (((1,), (1,)), ((), ()))
LIMIT = pltpu.CompilerParams(vmem_limit_bytes=16 * 2**20)


PIECES = ((0, 256), (256, 512), (512, 576))


def project_kernel(x_ref, wg_ref, wq_ref, out_ref, w_ref, acc_ref, sems):
    width, qw = wg_ref.shape[0], wq_ref.shape[0]
    total = width + qw
    copies = [
        pltpu.make_async_copy(wg_ref.at[pl.ds(lo, hi - lo)], w_ref.at[pl.ds(lo, hi - lo)], sems.at[i])
        for i, (lo, hi) in enumerate(PIECES)
    ]
    copies.append(pltpu.make_async_copy(wq_ref, w_ref.at[pl.ds(width, qw)], sems.at[3]))
    for c in copies:
        c.start()

    def put(part, lo, hi):
        for p in range(4):
            acc_ref[:, p * 8 : p * 8 + 8, lo:hi] = part[p * 64 : p * 64 + 64].reshape(8, 8, hi - lo)

    for i, (lo, hi) in enumerate(PIECES):
        copies[i].wait()
        if i == 2:
            copies[3].wait()
            hi = total
        part = lax.dot_general(x_ref[...], w_ref[lo:hi], NT, preferred_element_type=jnp.float32)
        put(part, lo, hi)
    query = part[:, PIECES[2][1] - PIECES[2][0] :]
    put(query - query.astype(jnp.bfloat16).astype(jnp.float32), total, total + qw)
    out_ref[...] = acc_ref[...].astype(jnp.bfloat16)


def project(rows, w_query, w_gate_up):
    d, _, width = w_gate_up.shape
    wg = w_gate_up.transpose(1, 2, 0).reshape(2 * width, d)
    wq = w_query.T
    total = 2 * width + wq.shape[0]
    shape = (8, rows.shape[0] // 8, total + wq.shape[0])
    vmem, hbm = pl.BlockSpec(memory_space=pltpu.VMEM), pl.BlockSpec(memory_space=pltpu.HBM)
    return pl.pallas_call(
        project_kernel,
        in_specs=[vmem, hbm, hbm],
        out_specs=vmem,
        out_shape=jax.ShapeDtypeStruct(shape, jnp.bfloat16),
        scratch_shapes=[
            pltpu.VMEM((total, d), jnp.bfloat16),
            pltpu.VMEM(shape, jnp.float32),
            pltpu.SemaphoreType.DMA((4,)),
        ],
        compiler_params=pltpu.CompilerParams(vmem_limit_bytes=52 * 2**20),
    )(rows, wg, wq)


def attend_kernel(order, place_ref, lengths_ref, q_ref, *refs):
    n = len(order)
    keys, values, (mine_ref, theirs_ref) = refs[:n], refs[n : 2 * n], refs[2 * n :]
    seqs, block_len, head_dim = keys[0].shape
    scale = head_dim ** (-0.5)
    slot = lax.broadcasted_iota(jnp.int32, (16, block_len), 1)
    for r in range(seqs):
        q = q_ref[r]
        scores, valid = [], []
        for j, flip in enumerate(order):
            s = lax.dot_general(q, keys[j][r], NT, preferred_element_type=jnp.float32) * scale
            start = jnp.bitwise_xor(place_ref[0], flip) * block_len
            valid.append(slot + start < lengths_ref[r])
            scores.append(jnp.where(valid[j], s, NEG))
        top = scores[0]
        for s in scores[1:]:
            top = jnp.maximum(top, s)
        top = jnp.max(top, axis=1, keepdims=True)
        total = jnp.zeros((16, 1), jnp.float32)
        mixed = jnp.zeros((16, head_dim), jnp.float32)
        for j in range(n):
            p = jnp.where(valid[j], jnp.exp(scores[j] - top), 0.0)
            total += jnp.sum(p, axis=1, keepdims=True)
            mixed += jnp.dot(p.astype(jnp.bfloat16), values[j][r], preferred_element_type=jnp.float32)
        for ref, rows in ((mine_ref, slice(0, 8)), (theirs_ref, slice(8, 16))):
            ref[r, :, :head_dim] = mixed[rows]
            lane = lax.broadcasted_iota(jnp.int32, (8, 128), 1)
            ref[r, :, head_dim:] = jnp.where(lane < 64, top[rows], total[rows])


def attend(place, lengths, queries, keys, values, order):
    seqs, _, head_dim = queries.shape
    smem, vmem = pl.BlockSpec(memory_space=pltpu.SMEM), pl.BlockSpec(memory_space=pltpu.VMEM)
    out = jax.ShapeDtypeStruct((seqs, 8, head_dim + 128), jnp.float32)

    def kernel(*refs):
        attend_kernel(order, *refs)

    return pl.pallas_call(
        kernel,
        in_specs=[smem, smem] + [vmem] * (1 + 2 * len(order)),
        out_specs=(vmem, vmem),
        out_shape=(out, out),
        compiler_params=LIMIT,
    )(place.reshape(1).astype(jnp.int32), lengths, queries, *keys, *values)


def finish_kernel(heads, mine_ref, theirs_ref, q_ref, new_ref, out_ref):
    seqs, _, head_dim = q_ref.shape
    scale = head_dim ** (-0.5)
    results = []
    for r in range(seqs):
        mine, theirs = mine_ref[r], theirs_ref[r]
        new = new_ref[r].astype(jnp.float32)
        q = q_ref[r].astype(jnp.float32)[:8]
        own = jnp.sum(q * new[0:1], axis=1, keepdims=True) * scale
        tops = [p[:, head_dim : head_dim + 1] for p in (mine, theirs)]
        sums = [p[:, head_dim + 64 : head_dim + 65] for p in (mine, theirs)]
        top = jnp.maximum(jnp.maximum(tops[0], tops[1]), own)
        w0, w1, w2 = jnp.exp(tops[0] - top), jnp.exp(tops[1] - top), jnp.exp(own - top)
        numer = mine[:, :head_dim] * w0 + theirs[:, :head_dim] * w1 + w2 * new[1:2]
        results.append(numer / (sums[0] * w0 + sums[1] * w1 + w2))
    for h in range(heads):
        rows = jnp.concatenate([x[h : h + 1] for x in results], axis=0)
        out_ref[:, h * head_dim : (h + 1) * head_dim] = rows.astype(jnp.bfloat16)


def finish(mine, theirs, queries, new_kv, heads):
    def kernel(*refs):
        finish_kernel(heads, *refs)

    seqs, _, head_dim = queries.shape
    return pl.pallas_call(
        kernel,
        out_shape=jax.ShapeDtypeStruct((seqs, heads * head_dim), jnp.bfloat16),
        compiler_params=LIMIT,
    )(mine, theirs, queries, new_kv)


def body(tokens, w_query, w_gate_up, key_cache, value_cache, new_kv, lengths):
    f32, bf16 = jnp.float32, jnp.bfloat16
    d, width, qw = tokens.shape[1], w_gate_up.shape[2], w_query.shape[1]
    seqs, _, head_dim = key_cache.shape

    keys_b, values_b = beside(key_cache), beside(value_cache)
    rows = spread(tokens, LATTICE, 32, far_groups()).reshape(64, d)
    rows, keys_b, values_b = lax.optimization_barrier((rows, keys_b, values_b))
    keys_c = other_core(key_cache)
    rows = spread(rows, PLANE, 4, near_groups()).reshape(256, d)
    rows, keys_c = lax.optimization_barrier((rows, keys_c))
    values_c, keys_d, values_d = other_core(value_cache), other_core(keys_b), other_core(values_b)

    got = exchange(project(rows, w_query, w_gate_up), GX)
    got, values_c, keys_d, values_d = lax.optimization_barrier((got, values_c, keys_d, values_d))
    got = got.astype(f32)
    total = jnp.sum(got, axis=0)
    hidden = (jax.nn.silu(total[:, :width]) * total[:, width : 2 * width]).astype(bf16)
    hidden = hidden.reshape(2, 2, 4, 2, width).transpose(0, 2, 1, 3, 4).reshape(32, width)
    query = (total[:, 2 * width : 2 * width + qw] + total[:, 2 * width + qw :]).astype(bf16)

    query = query.reshape(2, 2, 4, 2, qw).transpose(2, 1, 0, 3, 4).reshape(8, 4, qw)
    query = exchange(jnp.concatenate([query, query], axis=0), ALL, query_groups())
    place = lax.axis_index(GX)
    block = lax.axis_index("xh") * 4 + lax.axis_index("z") // 2
    sender = jnp.where(place == block, place % 2, (place < block).astype(place.dtype))
    query = lax.dynamic_slice_in_dim(query, sender * 8, 8, 0)
    query = query.reshape(8, 2, seqs, qw).transpose(1, 2, 0, 3).reshape(2, seqs, 8 * qw)
    query = jnp.concatenate([query, query], axis=0)
    query = exchange(query, ("xl", "z"), column_groups())
    per_dev = 16 * qw // head_dim
    query = query.reshape(2, 2, seqs, 8 * qw).transpose(0, 2, 1, 3).reshape(2, seqs, per_dev, head_dim)
    query = jnp.pad(query, ((0, 0), (0, 0), (0, 8 - per_dev), (0, 0)))
    upper = lax.axis_index("xl") >= 2
    own, other = jnp.where(upper, query[1], query[0]), jnp.where(upper, query[0], query[1])
    queries = jnp.concatenate([own, other], axis=1)

    keys = (key_cache, keys_b, keys_c, keys_d)
    values = (value_cache, values_b, values_c, values_d)
    mine, theirs = attend(place, lengths, queries, keys, values, (0, 2, 1, 3))
    attended = finish(mine, across(theirs), queries, new_kv, per_dev)
    return (hidden, attended)


def solution(mesh):
    fine = Mesh(mesh.devices.reshape(4, 2, 2, 8, 8), GX + GY)
    return jax.shard_map(
        body,
        mesh=fine,
        in_specs=(
            P(GY, GX),
            P(GX, GY),
            P(GX, None, GY),
            P(GY, GX, None),
            P(GY, GX, None),
            P(GY, None, None),
            P(GY),
        ),
        out_specs=(P(GX, GY), P(GY, GX)),
        check_vma=False,
    )
```

```python
import jax
import jax.numpy as jnp
from jax import lax
from jax.experimental import pallas as pl
from jax.experimental.pallas import tpu as pltpu
from jax.sharding import Mesh, PartitionSpec as P

NEG = -1e30
GX = ("xl", "core")
GY = ("xh", "z", "y")
ALL = GX + GY
PLANE = ("core", "z", "y")


def far_groups():
    return [
        [(zh * 2 + zlo) * 8 + yh * 2 + ylo for zh in range(4) for yh in range(4)] for zlo in range(2) for ylo in range(2)
    ]


def near_groups():
    groups = []
    for core in range(2):
        for zb in range(4):
            for yb in range(4):
                zs = sorted(((2 * zb + i + core) % 8 for i in range(2)), key=lambda v: v % 2)
                ys = sorted(((2 * yb + i + core) % 8 for i in range(2)), key=lambda v: v % 2)
                groups.append([core * 64 + z * 8 + y for z in zs for y in ys])
    return groups


def query_groups():
    def half(g, h):
        return [g * 128 + h * 16 + i for i in range(16)]

    pairs = [(g, h) for g in range(8) for h in range(g + 1, 8)]
    return [half(g, h) + half(h, g) for g, h in pairs] + [half(g, g) + half(g + 1, g + 1) for g in range(0, 8, 2)]


def exchange(x, axis, groups=None):
    return lax.all_to_all(x, axis, 0, 0, axis_index_groups=groups, tiled=True)


def spread(x, axis, n, groups=None):
    return exchange(jnp.broadcast_to(x[None], (n,) + x.shape), axis, groups)


def beside(x):
    return lax.ppermute(x, "xl", [(i, i ^ 1) for i in range(4)])


def across(x):
    return lax.ppermute(x, "xl", [(i, i ^ 2) for i in range(4)])


def other_core(x):
    return lax.ppermute(x, "core", [(0, 1), (1, 0)])


NT = (((1,), (1,)), ((), ()))
LIMIT = pltpu.CompilerParams(vmem_limit_bytes=16 * 2**20)


def project_kernel(x_ref, wg_ref, wq_ref, out_ref, acc_ref):
    n = x_ref.shape[0]
    i = lax.broadcasted_iota(jnp.int32, (n, n), 0)
    source = (i & ~63) | ((i >> 3 & 3) << 4) | ((i >> 1 & 3) << 2) | ((i >> 5 & 1) << 1) | (i & 1)
    order = (source == lax.broadcasted_iota(jnp.int32, (n, n), 1)).astype(jnp.float32).astype(jnp.bfloat16)
    x = jnp.dot(order, x_ref[...], preferred_element_type=jnp.float32).astype(jnp.bfloat16)
    width, qw = wg_ref.shape[0], wq_ref.shape[0]
    gate_up = lax.dot_general(x, wg_ref[...], NT, preferred_element_type=jnp.float32)
    query = lax.dot_general(x, wq_ref[...], NT, preferred_element_type=jnp.float32)
    for p in range(4):
        rows = slice(p * 64, p * 64 + 64)
        acc_ref[:, p * 8 : p * 8 + 8, :width] = gate_up[rows].reshape(8, 8, width)
        part = query[rows].reshape(8, 8, qw)
        acc_ref[:, p * 8 : p * 8 + 8, width : width + qw] = part
        acc_ref[:, p * 8 : p * 8 + 8, width + qw :] = part - part.astype(jnp.bfloat16).astype(jnp.float32)
    out_ref[...] = acc_ref[...].astype(jnp.bfloat16)


def project(rows, w_query, w_gate_up):
    d, _, width = w_gate_up.shape
    wg = w_gate_up.transpose(1, 2, 0).reshape(2 * width, d)
    wq = w_query.T
    shape = (8, rows.shape[0] // 8, 2 * width + 2 * wq.shape[0])
    return pl.pallas_call(
        project_kernel,
        out_shape=jax.ShapeDtypeStruct(shape, jnp.bfloat16),
        scratch_shapes=[pltpu.VMEM(shape, jnp.float32)],
        compiler_params=LIMIT,
    )(rows, wg, wq)


def attend_kernel(order, place_ref, lengths_ref, q_ref, *refs):
    n = len(order)
    keys, values, (mine_ref, theirs_ref) = refs[:n], refs[n : 2 * n], refs[2 * n :]
    seqs, block_len, head_dim = keys[0].shape
    scale = head_dim ** (-0.5)
    slot = lax.broadcasted_iota(jnp.int32, (16, block_len), 1)
    for r in range(seqs):
        q = q_ref[r]
        scores, valid = [], []
        for j, flip in enumerate(order):
            s = lax.dot_general(q, keys[j][r], NT, preferred_element_type=jnp.float32) * scale
            start = jnp.bitwise_xor(place_ref[0], flip) * block_len
            valid.append(slot + start < lengths_ref[r])
            scores.append(jnp.where(valid[j], s, NEG))
        top = scores[0]
        for s in scores[1:]:
            top = jnp.maximum(top, s)
        top = jnp.max(top, axis=1, keepdims=True)
        total = jnp.zeros((16, 1), jnp.float32)
        mixed = jnp.zeros((16, head_dim), jnp.float32)
        for j in range(n):
            p = jnp.where(valid[j], jnp.exp(scores[j] - top), 0.0)
            total += jnp.sum(p, axis=1, keepdims=True)
            mixed += jnp.dot(p.astype(jnp.bfloat16), values[j][r], preferred_element_type=jnp.float32)
        for ref, rows in ((mine_ref, slice(0, 8)), (theirs_ref, slice(8, 16))):
            ref[r, :, :head_dim] = mixed[rows]
            lane = lax.broadcasted_iota(jnp.int32, (8, 128), 1)
            ref[r, :, head_dim:] = jnp.where(lane < 64, top[rows], total[rows])


def attend(place, lengths, queries, keys, values, order):
    seqs, _, head_dim = queries.shape
    smem, vmem = pl.BlockSpec(memory_space=pltpu.SMEM), pl.BlockSpec(memory_space=pltpu.VMEM)
    out = jax.ShapeDtypeStruct((seqs, 8, head_dim + 128), jnp.float32)

    def kernel(*refs):
        attend_kernel(order, *refs)

    return pl.pallas_call(
        kernel,
        in_specs=[smem, smem] + [vmem] * (1 + 2 * len(order)),
        out_specs=(vmem, vmem),
        out_shape=(out, out),
        compiler_params=LIMIT,
    )(place.reshape(1).astype(jnp.int32), lengths, queries, *keys, *values)


def finish_kernel(heads, mine_ref, theirs_ref, q_ref, new_ref, out_ref):
    seqs, _, head_dim = q_ref.shape
    scale = head_dim ** (-0.5)
    results = []
    for r in range(seqs):
        mine, theirs = mine_ref[r], theirs_ref[r]
        new = new_ref[r].astype(jnp.float32)
        q = q_ref[r].astype(jnp.float32)[:8]
        own = jnp.sum(q * new[0:1], axis=1, keepdims=True) * scale
        tops = [p[:, head_dim : head_dim + 1] for p in (mine, theirs)]
        sums = [p[:, head_dim + 64 : head_dim + 65] for p in (mine, theirs)]
        top = jnp.maximum(jnp.maximum(tops[0], tops[1]), own)
        w0, w1, w2 = jnp.exp(tops[0] - top), jnp.exp(tops[1] - top), jnp.exp(own - top)
        numer = mine[:, :head_dim] * w0 + theirs[:, :head_dim] * w1 + w2 * new[1:2]
        results.append(numer / (sums[0] * w0 + sums[1] * w1 + w2))
    for h in range(heads):
        rows = jnp.concatenate([x[h : h + 1] for x in results], axis=0)
        out_ref[:, h * head_dim : (h + 1) * head_dim] = rows.astype(jnp.bfloat16)


def finish(mine, theirs, queries, new_kv, heads):
    def kernel(*refs):
        finish_kernel(heads, *refs)

    seqs, _, head_dim = queries.shape
    return pl.pallas_call(
        kernel,
        out_shape=jax.ShapeDtypeStruct((seqs, heads * head_dim), jnp.bfloat16),
        compiler_params=LIMIT,
    )(mine, theirs, queries, new_kv)


def body(tokens, w_query, w_gate_up, key_cache, value_cache, new_kv, lengths):
    f32, bf16 = jnp.float32, jnp.bfloat16
    d, width, qw = tokens.shape[1], w_gate_up.shape[2], w_query.shape[1]
    seqs, _, head_dim = key_cache.shape

    partner = lax.ppermute(tokens, "xh", [(0, 1), (1, 0)])
    first = lax.axis_index("xh") == 0
    rows = jnp.stack([jnp.where(first, tokens, partner), jnp.where(first, partner, tokens)])
    keys_b, values_b = beside(key_cache), beside(value_cache)
    rows = spread(rows.reshape(2 * seqs, d), ("z", "y"), 16, far_groups())
    rows = rows.reshape(64, d)
    rows, keys_b, values_b = lax.optimization_barrier((rows, keys_b, values_b))
    keys_c = other_core(key_cache)
    rows = spread(rows, PLANE, 4, near_groups()).reshape(256, d)
    rows, keys_c = lax.optimization_barrier((rows, keys_c))
    values_c, keys_d, values_d = other_core(value_cache), other_core(keys_b), other_core(values_b)

    got = exchange(project(rows, w_query, w_gate_up), GX).astype(f32)
    total = jnp.sum(got, axis=0)
    hidden = (jax.nn.silu(total[:, :width]) * total[:, width : 2 * width]).astype(bf16)
    hidden = hidden.reshape(2, 2, 4, 2, width).transpose(0, 2, 1, 3, 4).reshape(32, width)
    query = (total[:, 2 * width : 2 * width + qw] + total[:, 2 * width + qw :]).astype(bf16)

    query = query.reshape(2, 2, 4, 2, qw).transpose(0, 2, 1, 3, 4).reshape(16, 2, qw)
    query = exchange(jnp.concatenate([query, query], axis=0), ALL, query_groups())
    place = lax.axis_index(GX)
    block = lax.axis_index("xh") * 4 + lax.axis_index("z") // 2
    sender = jnp.where(place == block, place % 2, (place < block).astype(place.dtype))
    query = lax.dynamic_slice_in_dim(query, sender * 16, 16, 0)
    per_dev = 16 * qw // head_dim
    query = query.transpose(1, 0, 2).reshape(seqs, per_dev, head_dim)
    query = jnp.pad(query, ((0, 0), (0, 8 - per_dev), (0, 0)))
    queries = jnp.concatenate([query, across(query)], axis=1)

    keys = (key_cache, keys_b, keys_c, keys_d)
    values = (value_cache, values_b, values_c, values_d)
    mine, theirs = attend(place, lengths, queries, keys, values, (0, 2, 1, 3))
    attended = finish(mine, across(theirs), queries, new_kv, per_dev)
    return (hidden, attended)


def solution(mesh):
    fine = Mesh(mesh.devices.reshape(4, 2, 2, 8, 8), GX + GY)
    return jax.shard_map(
        body,
        mesh=fine,
        in_specs=(
            P(GY, GX),
            P(GX, GY),
            P(GX, None, GY),
            P(GY, GX, None),
            P(GY, GX, None),
            P(GY, None, None),
            P(GY),
        ),
        out_specs=(P(GX, GY), P(GY, GX)),
        check_vma=False,
    )
```

```python
import jax
import jax.numpy as jnp
from jax import lax
from jax.experimental import pallas as pl
from jax.experimental.pallas import tpu as pltpu
from jax.sharding import Mesh, PartitionSpec as P

NEG = -1e30
GX = ("xl", "core")
GY = ("xh", "z", "y")
LATTICE = ("xh", "z", "y")
PLANE = ("core", "z", "y")


def far_groups():
    return [
        [xh * 64 + (zh * 2 + zlo) * 8 + yh * 2 + ylo for xh in range(2) for zh in range(4) for yh in range(4)]
        for zlo in range(2)
        for ylo in range(2)
    ]


def near_groups():
    groups = []
    for core in range(2):
        for zb in range(4):
            for yb in range(4):
                zs = sorted(((2 * zb + i + core) % 8 for i in range(2)), key=lambda v: v % 2)
                ys = sorted(((2 * yb + i + core) % 8 for i in range(2)), key=lambda v: v % 2)
                groups.append([core * 64 + z * 8 + y for z in zs for y in ys])
    return groups


def column_groups():
    return [[zh * 16 + i for i in range(16)] for zh in range(4)]


def transposition(flip):
    return [(g * 16 + h * 2 + lo, (h ^ flip) * 16 + g * 2 + lo) for g in range(8) for h in range(8) for lo in range(2)]


def exchange(x, axis, groups=None):
    return lax.all_to_all(x, axis, 0, 0, axis_index_groups=groups, tiled=True)


def spread(x, axis, n, groups=None):
    return exchange(jnp.broadcast_to(x[None], (n,) + x.shape), axis, groups)


def beside(x):
    return lax.ppermute(x, "xl", [(i, i ^ 1) for i in range(4)])


def across(x):
    return lax.ppermute(x, "xl", [(i, i ^ 2) for i in range(4)])


def other_core(x):
    return lax.ppermute(x, "core", [(0, 1), (1, 0)])


NT = (((1,), (1,)), ((), ()))
LIMIT = pltpu.CompilerParams(vmem_limit_bytes=16 * 2**20)


def project_kernel(x_ref, wg_ref, wq_ref, out_ref, acc_ref):
    x = x_ref[...]
    width, qw = wg_ref.shape[0], wq_ref.shape[0]
    gate_up = lax.dot_general(x, wg_ref[...], NT, preferred_element_type=jnp.float32)
    query = lax.dot_general(x, wq_ref[...], NT, preferred_element_type=jnp.float32)
    for p in range(4):
        rows = slice(p * 64, p * 64 + 64)
        acc_ref[:, p * 8 : p * 8 + 8, :width] = gate_up[rows].reshape(8, 8, width)
        part = query[rows].reshape(8, 8, qw)
        acc_ref[:, p * 8 : p * 8 + 8, width : width + qw] = part
        acc_ref[:, p * 8 : p * 8 + 8, width + qw :] = part - part.astype(jnp.bfloat16).astype(jnp.float32)
    out_ref[...] = acc_ref[...].astype(jnp.bfloat16)


def project(rows, w_query, w_gate_up):
    d, _, width = w_gate_up.shape
    wg = w_gate_up.transpose(1, 2, 0).reshape(2 * width, d)
    wq = w_query.T
    shape = (8, rows.shape[0] // 8, 2 * width + 2 * wq.shape[0])
    return pl.pallas_call(
        project_kernel,
        out_shape=jax.ShapeDtypeStruct(shape, jnp.bfloat16),
        scratch_shapes=[pltpu.VMEM(shape, jnp.float32)],
        compiler_params=LIMIT,
    )(rows, wg, wq)


def attend_kernel(order, place_ref, lengths_ref, q_ref, *refs):
    n = len(order)
    keys, values, (mine_ref, theirs_ref) = refs[:n], refs[n : 2 * n], refs[2 * n :]
    seqs, block_len, head_dim = keys[0].shape
    scale = head_dim ** (-0.5)
    slot = lax.broadcasted_iota(jnp.int32, (16, block_len), 1)
    for r in range(seqs):
        q = q_ref[r]
        scores, valid = [], []
        for j, flip in enumerate(order):
            s = lax.dot_general(q, keys[j][r], NT, preferred_element_type=jnp.float32) * scale
            start = jnp.bitwise_xor(place_ref[0], flip) * block_len
            valid.append(slot + start < lengths_ref[r])
            scores.append(jnp.where(valid[j], s, NEG))
        top = scores[0]
        for s in scores[1:]:
            top = jnp.maximum(top, s)
        top = jnp.max(top, axis=1, keepdims=True)
        total = jnp.zeros((16, 1), jnp.float32)
        mixed = jnp.zeros((16, head_dim), jnp.float32)
        for j in range(n):
            p = jnp.where(valid[j], jnp.exp(scores[j] - top), 0.0)
            total += jnp.sum(p, axis=1, keepdims=True)
            mixed += jnp.dot(p.astype(jnp.bfloat16), values[j][r], preferred_element_type=jnp.float32)
        for ref, rows in ((mine_ref, slice(0, 8)), (theirs_ref, slice(8, 16))):
            ref[r, :, :head_dim] = mixed[rows]
            lane = lax.broadcasted_iota(jnp.int32, (8, 128), 1)
            ref[r, :, head_dim:] = jnp.where(lane < 64, top[rows], total[rows])


def attend(place, lengths, queries, keys, values, order):
    seqs, _, head_dim = queries.shape
    smem, vmem = pl.BlockSpec(memory_space=pltpu.SMEM), pl.BlockSpec(memory_space=pltpu.VMEM)
    out = jax.ShapeDtypeStruct((seqs, 8, head_dim + 128), jnp.float32)

    def kernel(*refs):
        attend_kernel(order, *refs)

    return pl.pallas_call(
        kernel,
        in_specs=[smem, smem] + [vmem] * (1 + 2 * len(order)),
        out_specs=(vmem, vmem),
        out_shape=(out, out),
        compiler_params=LIMIT,
    )(place.reshape(1).astype(jnp.int32), lengths, queries, *keys, *values)


def finish_kernel(heads, mine_ref, theirs_ref, q_ref, new_ref, out_ref):
    seqs, _, head_dim = q_ref.shape
    scale = head_dim ** (-0.5)
    results = []
    for r in range(seqs):
        mine, theirs = mine_ref[r], theirs_ref[r]
        new = new_ref[r].astype(jnp.float32)
        q = q_ref[r].astype(jnp.float32)[:8]
        own = jnp.sum(q * new[0:1], axis=1, keepdims=True) * scale
        tops = [p[:, head_dim : head_dim + 1] for p in (mine, theirs)]
        sums = [p[:, head_dim + 64 : head_dim + 65] for p in (mine, theirs)]
        top = jnp.maximum(jnp.maximum(tops[0], tops[1]), own)
        w0, w1, w2 = jnp.exp(tops[0] - top), jnp.exp(tops[1] - top), jnp.exp(own - top)
        numer = mine[:, :head_dim] * w0 + theirs[:, :head_dim] * w1 + w2 * new[1:2]
        results.append(numer / (sums[0] * w0 + sums[1] * w1 + w2))
    for h in range(heads):
        rows = jnp.concatenate([x[h : h + 1] for x in results], axis=0)
        out_ref[:, h * head_dim : (h + 1) * head_dim] = rows.astype(jnp.bfloat16)


def finish(mine, theirs, queries, new_kv, heads):
    def kernel(*refs):
        finish_kernel(heads, *refs)

    seqs, _, head_dim = queries.shape
    return pl.pallas_call(
        kernel,
        out_shape=jax.ShapeDtypeStruct((seqs, heads * head_dim), jnp.bfloat16),
        compiler_params=LIMIT,
    )(mine, theirs, queries, new_kv)


def body(tokens, w_query, w_gate_up, key_cache, value_cache, new_kv, lengths):
    f32, bf16 = jnp.float32, jnp.bfloat16
    d, width, qw = tokens.shape[1], w_gate_up.shape[2], w_query.shape[1]
    seqs, _, head_dim = key_cache.shape

    keys_b = beside(key_cache)
    rows = spread(tokens, LATTICE, 32, far_groups()).reshape(64, d)
    rows, keys_b = lax.optimization_barrier((rows, keys_b))
    values_b, keys_c = beside(value_cache), other_core(key_cache)
    rows = spread(rows, PLANE, 4, near_groups()).reshape(256, d)
    rows, values_b, keys_c = lax.optimization_barrier((rows, values_b, keys_c))
    values_c, keys_d, values_d = other_core(value_cache), other_core(keys_b), other_core(values_b)

    got = exchange(project(rows, w_query, w_gate_up), GX).astype(f32)
    total = jnp.sum(got, axis=0)
    hidden = (jax.nn.silu(total[:, :width]) * total[:, width : 2 * width]).astype(bf16)
    hidden = hidden.reshape(2, 2, 4, 2, width).transpose(0, 2, 1, 3, 4).reshape(32, width)
    query = (total[:, 2 * width : 2 * width + qw] + total[:, 2 * width + qw :]).astype(bf16)

    query = query.reshape(2, 2, 4, 2, qw).transpose(0, 2, 1, 3, 4).reshape(16, seqs, qw)
    query = exchange(query, ("z", "y"), column_groups())
    per_dev = 16 * qw // head_dim
    query = query.transpose(1, 0, 2).reshape(seqs, per_dev, head_dim)
    query = jnp.pad(query, ((0, 0), (0, 8 - per_dev), (0, 0)))
    queries = [lax.ppermute(query, ("xl", "core", "xh", "z"), transposition(flip)) for flip in (0, 4)]
    queries = jnp.concatenate(queries, axis=1)
    place = lax.axis_index(GX)

    keys = (key_cache, keys_b, keys_c, keys_d)
    values = (value_cache, values_b, values_c, values_d)
    mine, theirs = attend(place, lengths, queries, keys, values, (0, 2, 1, 3))
    attended = finish(mine, across(theirs), queries, new_kv, per_dev)
    return (hidden, attended)


def solution(mesh):
    fine = Mesh(mesh.devices.reshape(4, 2, 2, 8, 8), GX + GY)
    return jax.shard_map(
        body,
        mesh=fine,
        in_specs=(
            P(GY, GX),
            P(GX, GY),
            P(GX, None, GY),
            P(GY, GX, None),
            P(GY, GX, None),
            P(GY, None, None),
            P(GY),
        ),
        out_specs=(P(GX, GY), P(GY, GX)),
        check_vma=False,
    )
```

```python
import jax
import jax.numpy as jnp
from jax import lax
from jax.experimental import pallas as pl
from jax.experimental.pallas import tpu as pltpu
from jax.sharding import Mesh, PartitionSpec as P

NEG = -1e30
GX = ("xl", "core")
GY = ("xh", "z", "y")
ALL = GX + GY
LATTICE = ("xh", "z", "y")
PLANE = ("core", "z", "y")


def far_groups():
    return [
        [xh * 64 + (zh * 2 + zlo) * 8 + yh * 2 + ylo for xh in range(2) for zh in range(4) for yh in range(4)]
        for zlo in range(2)
        for ylo in range(2)
    ]


def near_groups():
    groups = []
    for core in range(2):
        for zb in range(4):
            for yb in range(4):
                zs = sorted(((2 * zb + i + core) % 8 for i in range(2)), key=lambda v: v % 2)
                ys = sorted(((2 * yb + i + core) % 8 for i in range(2)), key=lambda v: v % 2)
                groups.append([core * 64 + z * 8 + y for z in zs for y in ys])
    return groups


def query_groups():
    def half(g, h):
        return [g * 128 + h * 16 + i for i in range(16)]

    pairs = [(g, h) for g in range(8) for h in range(g + 1, 8)]
    return [half(g, h) + half(h, g) for g, h in pairs] + [half(g, g) + half(g + 1, g + 1) for g in range(0, 8, 2)]


def exchange(x, axis, groups=None):
    return lax.all_to_all(x, axis, 0, 0, axis_index_groups=groups, tiled=True)


def spread(x, axis, n, groups=None):
    return exchange(jnp.broadcast_to(x[None], (n,) + x.shape), axis, groups)


def beside(x):
    return lax.ppermute(x, "xl", [(i, i ^ 1) for i in range(4)])


def across(x):
    return lax.ppermute(x, "xl", [(i, i ^ 2) for i in range(4)])


def other_core(x):
    return lax.ppermute(x, "core", [(0, 1), (1, 0)])


NT = (((1,), (1,)), ((), ()))
LIMIT = pltpu.CompilerParams(vmem_limit_bytes=16 * 2**20)


def project_kernel(x_ref, wg_ref, wq_ref, out_ref, acc_ref):
    x = x_ref[...]
    width, qw = wg_ref.shape[0], wq_ref.shape[0]
    gate_up = lax.dot_general(x, wg_ref[...], NT, preferred_element_type=jnp.float32)
    query = lax.dot_general(x, wq_ref[...], NT, preferred_element_type=jnp.float32)
    for p in range(4):
        rows = slice(p * 64, p * 64 + 64)
        acc_ref[:, p * 8 : p * 8 + 8, :width] = gate_up[rows].reshape(8, 8, width)
        part = query[rows].reshape(8, 8, qw)
        acc_ref[:, p * 8 : p * 8 + 8, width : width + qw] = part
        acc_ref[:, p * 8 : p * 8 + 8, width + qw :] = part - part.astype(jnp.bfloat16).astype(jnp.float32)
    out_ref[...] = acc_ref[...].astype(jnp.bfloat16)


def project(rows, w_query, w_gate_up):
    d, _, width = w_gate_up.shape
    wg = w_gate_up.transpose(1, 2, 0).reshape(2 * width, d)
    wq = w_query.T
    shape = (8, rows.shape[0] // 8, 2 * width + 2 * wq.shape[0])
    return pl.pallas_call(
        project_kernel,
        out_shape=jax.ShapeDtypeStruct(shape, jnp.bfloat16),
        scratch_shapes=[pltpu.VMEM(shape, jnp.float32)],
        compiler_params=LIMIT,
    )(rows, wg, wq)


def attend_kernel(order, place_ref, lengths_ref, q_ref, *refs):
    n = len(order)
    keys, values, out_ref = refs[:n], refs[n : 2 * n], refs[2 * n]
    seqs, block_len, head_dim = keys[0].shape
    scale = head_dim ** (-0.5)
    slot = lax.broadcasted_iota(jnp.int32, (8, block_len), 1)
    lane = lax.broadcasted_iota(jnp.int32, (8, 128), 1)
    for r in range(seqs):
        q = q_ref[r]
        scores, valid = [], []
        for j, flip in enumerate(order):
            s = lax.dot_general(q, keys[j][r], NT, preferred_element_type=jnp.float32) * scale
            start = jnp.bitwise_xor(place_ref[0], flip) * block_len
            valid.append(slot + start < lengths_ref[r])
            scores.append(jnp.where(valid[j], s, NEG))
        top = scores[0]
        for s in scores[1:]:
            top = jnp.maximum(top, s)
        top = jnp.max(top, axis=1, keepdims=True)
        probs = [jnp.where(ok, jnp.exp(s - top), 0.0) for s, ok in zip(scores, valid)]
        total = probs[0]
        for p in probs[1:]:
            total = total + p
        total = jnp.sum(total, axis=1, keepdims=True)
        mixed = jnp.zeros((8, head_dim), jnp.float32)
        for p, v in zip(probs, values):
            mixed += jnp.dot(p.astype(jnp.bfloat16), v[r], preferred_element_type=jnp.float32)
        out_ref[r, :, :head_dim] = mixed
        out_ref[r, :, head_dim:] = jnp.where(lane < 64, top, total)


def attend(place, lengths, queries, keys, values, order):
    seqs, _, head_dim = queries.shape
    smem, vmem = pl.BlockSpec(memory_space=pltpu.SMEM), pl.BlockSpec(memory_space=pltpu.VMEM)

    def kernel(*refs):
        attend_kernel(order, *refs)

    return pl.pallas_call(
        kernel,
        in_specs=[smem, smem] + [vmem] * (1 + 2 * len(order)),
        out_specs=vmem,
        out_shape=jax.ShapeDtypeStruct((seqs, 8, head_dim + 128), jnp.float32),
        compiler_params=LIMIT,
    )(place.reshape(1).astype(jnp.int32), lengths, queries, *keys, *values)


def finish_kernel(heads, mine_ref, theirs_ref, q_ref, new_ref, out_ref):
    seqs, _, head_dim = q_ref.shape
    scale = head_dim ** (-0.5)
    results = []
    for r in range(seqs):
        mine, theirs = mine_ref[r], theirs_ref[r]
        new = new_ref[r].astype(jnp.float32)
        q = q_ref[r].astype(jnp.float32)
        own = jnp.sum(q * new[0:1], axis=1, keepdims=True) * scale
        tops = [p[:, head_dim : head_dim + 1] for p in (mine, theirs)]
        sums = [p[:, head_dim + 64 : head_dim + 65] for p in (mine, theirs)]
        top = jnp.maximum(jnp.maximum(tops[0], tops[1]), own)
        w0, w1, w2 = jnp.exp(tops[0] - top), jnp.exp(tops[1] - top), jnp.exp(own - top)
        numer = mine[:, :head_dim] * w0 + theirs[:, :head_dim] * w1 + w2 * new[1:2]
        results.append(numer / (sums[0] * w0 + sums[1] * w1 + w2))
    for h in range(heads):
        rows = jnp.concatenate([x[h : h + 1] for x in results], axis=0)
        out_ref[:, h * head_dim : (h + 1) * head_dim] = rows.astype(jnp.bfloat16)


def finish(mine, theirs, queries, new_kv, heads):
    def kernel(*refs):
        finish_kernel(heads, *refs)

    seqs, _, head_dim = queries.shape
    return pl.pallas_call(
        kernel,
        out_shape=jax.ShapeDtypeStruct((seqs, heads * head_dim), jnp.bfloat16),
        compiler_params=LIMIT,
    )(mine, theirs, queries, new_kv)


def body(tokens, w_query, w_gate_up, key_cache, value_cache, new_kv, lengths):
    f32, bf16 = jnp.float32, jnp.bfloat16
    d, width, qw = tokens.shape[1], w_gate_up.shape[2], w_query.shape[1]
    seqs, _, head_dim = key_cache.shape

    keys_b = beside(key_cache)
    rows = spread(tokens, LATTICE, 32, far_groups()).reshape(64, d)
    rows, keys_b = lax.optimization_barrier((rows, keys_b))
    values_b, keys_c = beside(value_cache), other_core(key_cache)
    rows = spread(rows, PLANE, 4, near_groups()).reshape(256, d)
    rows, values_b, keys_c = lax.optimization_barrier((rows, values_b, keys_c))
    values_c, keys_d, values_d = other_core(value_cache), other_core(keys_b), other_core(values_b)

    got = exchange(project(rows, w_query, w_gate_up), GX).astype(f32)
    total = jnp.sum(got, axis=0)
    hidden = (jax.nn.silu(total[:, :width]) * total[:, width : 2 * width]).astype(bf16)
    hidden = hidden.reshape(2, 2, 4, 2, width).transpose(0, 2, 1, 3, 4).reshape(32, width)
    query = (total[:, 2 * width : 2 * width + qw] + total[:, 2 * width + qw :]).astype(bf16)

    query = query.reshape(2, 2, 4, 2, qw).transpose(0, 2, 1, 3, 4).reshape(16, 2, qw)
    query = exchange(jnp.concatenate([query, query], axis=0), ALL, query_groups())
    place = lax.axis_index(GX)
    block = lax.axis_index("xh") * 4 + lax.axis_index("z") // 2
    sender = jnp.where(place == block, place % 2, (place < block).astype(place.dtype))
    query = lax.dynamic_slice_in_dim(query, sender * 16, 16, 0)
    per_dev = 16 * qw // head_dim
    query = query.transpose(1, 0, 2).reshape(seqs, per_dev, head_dim)
    query = jnp.pad(query, ((0, 0), (0, 8 - per_dev), (0, 0)))

    keys = (key_cache, keys_b, keys_c, keys_d)
    values = (value_cache, values_b, values_c, values_d)
    mine = attend(place, lengths, query, keys, values, (0, 2, 1, 3))
    theirs = attend(place, lengths, across(query), keys, values, (0, 2, 1, 3))
    attended = finish(mine, across(theirs), query, new_kv, per_dev)
    return (hidden, attended)


def solution(mesh):
    fine = Mesh(mesh.devices.reshape(4, 2, 2, 8, 8), GX + GY)
    return jax.shard_map(
        body,
        mesh=fine,
        in_specs=(
            P(GY, GX),
            P(GX, GY),
            P(GX, None, GY),
            P(GY, GX, None),
            P(GY, GX, None),
            P(GY, None, None),
            P(GY),
        ),
        out_specs=(P(GX, GY), P(GY, GX)),
        check_vma=False,
    )
```

```python
import jax
import jax.numpy as jnp
from jax import lax
from jax.experimental import pallas as pl
from jax.experimental.pallas import tpu as pltpu
from jax.sharding import Mesh, PartitionSpec as P

NEG = -1e30
GX = ("xl", "core")
GY = ("xh", "z", "y")
ALL = GX + GY
LATTICE = ("xh", "z", "y")
PLANE = ("core", "z", "y")


def far_groups():
    return [
        [xh * 64 + (zh * 2 + zlo) * 8 + yh * 2 + ylo for xh in range(2) for zh in range(4) for yh in range(4)]
        for zlo in range(2)
        for ylo in range(2)
    ]


def near_groups():
    groups = []
    for core in range(2):
        for zb in range(4):
            for yb in range(4):
                zs = sorted(((2 * zb + i + core) % 8 for i in range(2)), key=lambda v: v % 2)
                ys = sorted(((2 * yb + i + core) % 8 for i in range(2)), key=lambda v: v % 2)
                groups.append([core * 64 + z * 8 + y for z in zs for y in ys])
    return groups


def query_groups():
    def half(g, h):
        return [g * 128 + h * 16 + i for i in range(16)]

    pairs = [(g, h) for g in range(8) for h in range(g + 1, 8)]
    return [half(g, h) + half(h, g) for g, h in pairs] + [half(g, g) + half(g + 1, g + 1) for g in range(0, 8, 2)]


def exchange(x, axis, groups=None):
    return lax.all_to_all(x, axis, 0, 0, axis_index_groups=groups, tiled=True)


def spread(x, axis, n, groups=None):
    return exchange(jnp.broadcast_to(x[None], (n,) + x.shape), axis, groups)


def beside(x):
    return lax.ppermute(x, "xl", [(i, i ^ 1) for i in range(4)])


def across(x):
    return lax.ppermute(x, "xl", [(i, i ^ 2) for i in range(4)])


def other_core(x):
    return lax.ppermute(x, "core", [(0, 1), (1, 0)])


NT = (((1,), (1,)), ((), ()))
LIMIT = pltpu.CompilerParams(vmem_limit_bytes=16 * 2**20)


def project_kernel(low, x_ref, w_ref, out_ref, acc_ref):
    full = lax.dot_general(x_ref[...], w_ref[...], NT, preferred_element_type=jnp.float32)
    width = full.shape[1]
    for p in range(4):
        part = full[p * 64 : p * 64 + 64].reshape(8, 8, width)
        acc_ref[:, p * 8 : p * 8 + 8, :width] = part
        if low:
            acc_ref[:, p * 8 : p * 8 + 8, width:] = part - part.astype(jnp.bfloat16).astype(jnp.float32)
    out_ref[...] = acc_ref[...].astype(jnp.bfloat16)


def project(rows, weights, low):
    def kernel(*refs):
        project_kernel(low, *refs)

    shape = (8, rows.shape[0] // 8, weights.shape[0] * (1 + low))
    return pl.pallas_call(
        kernel,
        out_shape=jax.ShapeDtypeStruct(shape, jnp.bfloat16),
        scratch_shapes=[pltpu.VMEM(shape, jnp.float32)],
        compiler_params=LIMIT,
    )(rows, weights)


def attend_kernel(order, place_ref, lengths_ref, q_ref, *refs):
    n = len(order)
    keys, values, (mine_ref, theirs_ref) = refs[:n], refs[n : 2 * n], refs[2 * n :]
    seqs, block_len, head_dim = keys[0].shape
    scale = head_dim ** (-0.5)
    slot = lax.broadcasted_iota(jnp.int32, (16, block_len), 1)
    for r in range(seqs):
        q = q_ref[r]
        scores, valid = [], []
        for j, flip in enumerate(order):
            s = lax.dot_general(q, keys[j][r], NT, preferred_element_type=jnp.float32) * scale
            start = jnp.bitwise_xor(place_ref[0], flip) * block_len
            valid.append(slot + start < lengths_ref[r])
            scores.append(jnp.where(valid[j], s, NEG))
        top = scores[0]
        for s in scores[1:]:
            top = jnp.maximum(top, s)
        top = jnp.max(top, axis=1, keepdims=True)
        total = jnp.zeros((16, 1), jnp.float32)
        mixed = jnp.zeros((16, head_dim), jnp.float32)
        for j in range(n):
            p = jnp.where(valid[j], jnp.exp(scores[j] - top), 0.0)
            total += jnp.sum(p, axis=1, keepdims=True)
            mixed += jnp.dot(p.astype(jnp.bfloat16), values[j][r], preferred_element_type=jnp.float32)
        for ref, rows in ((mine_ref, slice(0, 8)), (theirs_ref, slice(8, 16))):
            ref[r, :, :head_dim] = mixed[rows]
            lane = lax.broadcasted_iota(jnp.int32, (8, 128), 1)
            ref[r, :, head_dim:] = jnp.where(lane < 64, top[rows], total[rows])


def attend(place, lengths, queries, keys, values, order):
    seqs, _, head_dim = queries.shape
    smem, vmem = pl.BlockSpec(memory_space=pltpu.SMEM), pl.BlockSpec(memory_space=pltpu.VMEM)
    out = jax.ShapeDtypeStruct((seqs, 8, head_dim + 128), jnp.float32)

    def kernel(*refs):
        attend_kernel(order, *refs)

    return pl.pallas_call(
        kernel,
        in_specs=[smem, smem] + [vmem] * (1 + 2 * len(order)),
        out_specs=(vmem, vmem),
        out_shape=(out, out),
        compiler_params=LIMIT,
    )(place.reshape(1).astype(jnp.int32), lengths, queries, *keys, *values)


def finish_kernel(heads, mine_ref, theirs_ref, q_ref, new_ref, out_ref):
    seqs, _, head_dim = q_ref.shape
    scale = head_dim ** (-0.5)
    results = []
    for r in range(seqs):
        mine, theirs = mine_ref[r], theirs_ref[r]
        new = new_ref[r].astype(jnp.float32)
        q = q_ref[r].astype(jnp.float32)[:8]
        own = jnp.sum(q * new[0:1], axis=1, keepdims=True) * scale
        tops = [p[:, head_dim : head_dim + 1] for p in (mine, theirs)]
        sums = [p[:, head_dim + 64 : head_dim + 65] for p in (mine, theirs)]
        top = jnp.maximum(jnp.maximum(tops[0], tops[1]), own)
        w0, w1, w2 = jnp.exp(tops[0] - top), jnp.exp(tops[1] - top), jnp.exp(own - top)
        numer = mine[:, :head_dim] * w0 + theirs[:, :head_dim] * w1 + w2 * new[1:2]
        results.append(numer / (sums[0] * w0 + sums[1] * w1 + w2))
    for h in range(heads):
        rows = jnp.concatenate([x[h : h + 1] for x in results], axis=0)
        out_ref[:, h * head_dim : (h + 1) * head_dim] = rows.astype(jnp.bfloat16)


def finish(mine, theirs, queries, new_kv, heads):
    def kernel(*refs):
        finish_kernel(heads, *refs)

    seqs, _, head_dim = queries.shape
    return pl.pallas_call(
        kernel,
        out_shape=jax.ShapeDtypeStruct((seqs, heads * head_dim), jnp.bfloat16),
        compiler_params=LIMIT,
    )(mine, theirs, queries, new_kv)


def body(tokens, w_query, w_gate_up, key_cache, value_cache, new_kv, lengths):
    f32, bf16 = jnp.float32, jnp.bfloat16
    d, width, qw = tokens.shape[1], w_gate_up.shape[2], w_query.shape[1]
    seqs, _, head_dim = key_cache.shape

    keys_b, keys_c = beside(key_cache), other_core(key_cache)
    rows = spread(tokens, LATTICE, 32, far_groups()).reshape(64, d)
    rows, keys_b, keys_c = lax.optimization_barrier((rows, keys_b, keys_c))
    values_b = beside(value_cache)
    rows = spread(rows, PLANE, 4, near_groups()).reshape(256, d)
    rows, values_b = lax.optimization_barrier((rows, values_b))
    values_c, keys_d, values_d = other_core(value_cache), other_core(keys_b), other_core(values_b)

    got = exchange(project(rows, w_query.T, True), GX)
    got, values_c, keys_d = lax.optimization_barrier((got, values_c, keys_d))
    total = jnp.sum(got.astype(f32), axis=0)
    query = (total[:, :qw] + total[:, qw:]).astype(bf16)

    query = query.reshape(2, 2, 4, 2, qw).transpose(0, 2, 1, 3, 4).reshape(16, 2, qw)
    query = exchange(jnp.concatenate([query, query], axis=0), ALL, query_groups())
    gate_up = project(rows, w_gate_up.transpose(1, 2, 0).reshape(2 * width, d), False)
    query, gate_up, values_d = lax.optimization_barrier((query, gate_up, values_d))
    place = lax.axis_index(GX)
    block = lax.axis_index("xh") * 4 + lax.axis_index("z") // 2
    sender = jnp.where(place == block, place % 2, (place < block).astype(place.dtype))
    query = lax.dynamic_slice_in_dim(query, sender * 16, 16, 0)
    per_dev = 16 * qw // head_dim
    query = query.transpose(1, 0, 2).reshape(seqs, per_dev, head_dim)
    query = jnp.pad(query, ((0, 0), (0, 8 - per_dev), (0, 0)))
    queries = jnp.concatenate([query, across(query)], axis=1)

    keys = (key_cache, keys_b, keys_c, keys_d)
    values = (value_cache, values_b, values_c, values_d)
    mine, theirs = attend(place, lengths, queries, keys, values, (0, 2, 1, 3))
    attended = finish(mine, across(theirs), queries, new_kv, per_dev)
    total = jnp.sum(exchange(gate_up, GX).astype(f32), axis=0)
    hidden = (jax.nn.silu(total[:, :width]) * total[:, width:]).astype(bf16)
    hidden = hidden.reshape(2, 2, 4, 2, width).transpose(0, 2, 1, 3, 4).reshape(32, width)
    return (hidden, attended)


def solution(mesh):
    fine = Mesh(mesh.devices.reshape(4, 2, 2, 8, 8), GX + GY)
    return jax.shard_map(
        body,
        mesh=fine,
        in_specs=(
            P(GY, GX),
            P(GX, GY),
            P(GX, None, GY),
            P(GY, GX, None),
            P(GY, GX, None),
            P(GY, None, None),
            P(GY),
        ),
        out_specs=(P(GX, GY), P(GY, GX)),
        check_vma=False,
    )
```

```python
import jax
import jax.numpy as jnp
from jax import lax
from jax.experimental import pallas as pl
from jax.experimental.pallas import tpu as pltpu
from jax.sharding import Mesh, PartitionSpec as P

NEG = -1e30
GX = ("xl", "core")
GY = ("xh", "z", "y")
ALL = GX + GY
LATTICE = ("xh", "z", "y")
PLANE = ("core", "z", "y")


def far_groups():
    return [
        [xh * 64 + (zh * 2 + zlo) * 8 + yh * 2 + ylo for xh in range(2) for zh in range(4) for yh in range(4)]
        for zlo in range(2)
        for ylo in range(2)
    ]


def near_groups():
    groups = []
    for core in range(2):
        for zb in range(4):
            for yb in range(4):
                zs = sorted(((2 * zb + i + core) % 8 for i in range(2)), key=lambda v: v % 2)
                ys = sorted(((2 * yb + i + core) % 8 for i in range(2)), key=lambda v: v % 2)
                groups.append([core * 64 + z * 8 + y for z in zs for y in ys])
    return groups


def query_groups():
    def half(g, h):
        return [g * 128 + h * 16 + i for i in range(16)]

    pairs = [(g, h) for g in range(8) for h in range(g + 1, 8)]
    return [half(g, h) + half(h, g) for g, h in pairs] + [half(g, g) + half(g + 1, g + 1) for g in range(0, 8, 2)]


def exchange(x, axis, groups=None):
    return lax.all_to_all(x, axis, 0, 0, axis_index_groups=groups, tiled=True)


def spread(x, axis, n, groups=None):
    return exchange(jnp.broadcast_to(x[None], (n,) + x.shape), axis, groups)


def beside(x):
    return lax.ppermute(x, "xl", [(i, i ^ 1) for i in range(4)])


def across(x):
    return lax.ppermute(x, "xl", [(i, i ^ 2) for i in range(4)])


def other_core(x):
    return lax.ppermute(x, "core", [(0, 1), (1, 0)])


NT = (((1,), (1,)), ((), ()))
LIMIT = pltpu.CompilerParams(vmem_limit_bytes=16 * 2**20)


def project_kernel(low, x_ref, w_ref, out_ref, acc_ref):
    full = lax.dot_general(x_ref[...], w_ref[...], NT, preferred_element_type=jnp.float32)
    width = full.shape[1]
    for p in range(4):
        part = full[p * 64 : p * 64 + 64].reshape(8, 8, width)
        acc_ref[:, p * 8 : p * 8 + 8, :width] = part
        if low:
            acc_ref[:, p * 8 : p * 8 + 8, width:] = part - part.astype(jnp.bfloat16).astype(jnp.float32)
    out_ref[...] = acc_ref[...].astype(jnp.bfloat16)


def project(rows, weights, low):
    def kernel(*refs):
        project_kernel(low, *refs)

    shape = (8, rows.shape[0] // 8, weights.shape[0] * (1 + low))
    return pl.pallas_call(
        kernel,
        out_shape=jax.ShapeDtypeStruct(shape, jnp.bfloat16),
        scratch_shapes=[pltpu.VMEM(shape, jnp.float32)],
        compiler_params=LIMIT,
    )(rows, weights)


def attend_kernel(order, place_ref, lengths_ref, q_ref, *refs):
    n = len(order)
    keys, values, (mine_ref, theirs_ref) = refs[:n], refs[n : 2 * n], refs[2 * n :]
    seqs, block_len, head_dim = keys[0].shape
    scale = head_dim ** (-0.5)
    slot = lax.broadcasted_iota(jnp.int32, (16, block_len), 1)
    for r in range(seqs):
        q = q_ref[r]
        scores, valid = [], []
        for j, flip in enumerate(order):
            s = lax.dot_general(q, keys[j][r], NT, preferred_element_type=jnp.float32) * scale
            start = jnp.bitwise_xor(place_ref[0], flip) * block_len
            valid.append(slot + start < lengths_ref[r])
            scores.append(jnp.where(valid[j], s, NEG))
        top = scores[0]
        for s in scores[1:]:
            top = jnp.maximum(top, s)
        top = jnp.max(top, axis=1, keepdims=True)
        total = jnp.zeros((16, 1), jnp.float32)
        mixed = jnp.zeros((16, head_dim), jnp.float32)
        for j in range(n):
            p = jnp.where(valid[j], jnp.exp(scores[j] - top), 0.0)
            total += jnp.sum(p, axis=1, keepdims=True)
            mixed += jnp.dot(p.astype(jnp.bfloat16), values[j][r], preferred_element_type=jnp.float32)
        for ref, rows in ((mine_ref, slice(0, 8)), (theirs_ref, slice(8, 16))):
            ref[r, :, :head_dim] = mixed[rows]
            lane = lax.broadcasted_iota(jnp.int32, (8, 128), 1)
            ref[r, :, head_dim:] = jnp.where(lane < 64, top[rows], total[rows])


def attend(place, lengths, queries, keys, values, order):
    seqs, _, head_dim = queries.shape
    smem, vmem = pl.BlockSpec(memory_space=pltpu.SMEM), pl.BlockSpec(memory_space=pltpu.VMEM)
    out = jax.ShapeDtypeStruct((seqs, 8, head_dim + 128), jnp.float32)

    def kernel(*refs):
        attend_kernel(order, *refs)

    return pl.pallas_call(
        kernel,
        in_specs=[smem, smem] + [vmem] * (1 + 2 * len(order)),
        out_specs=(vmem, vmem),
        out_shape=(out, out),
        compiler_params=LIMIT,
    )(place.reshape(1).astype(jnp.int32), lengths, queries, *keys, *values)


def finish_kernel(heads, mine_ref, theirs_ref, q_ref, new_ref, out_ref):
    seqs, _, head_dim = q_ref.shape
    scale = head_dim ** (-0.5)
    results = []
    for r in range(seqs):
        mine, theirs = mine_ref[r], theirs_ref[r]
        new = new_ref[r].astype(jnp.float32)
        q = q_ref[r].astype(jnp.float32)[:8]
        own = jnp.sum(q * new[0:1], axis=1, keepdims=True) * scale
        tops = [p[:, head_dim : head_dim + 1] for p in (mine, theirs)]
        sums = [p[:, head_dim + 64 : head_dim + 65] for p in (mine, theirs)]
        top = jnp.maximum(jnp.maximum(tops[0], tops[1]), own)
        w0, w1, w2 = jnp.exp(tops[0] - top), jnp.exp(tops[1] - top), jnp.exp(own - top)
        numer = mine[:, :head_dim] * w0 + theirs[:, :head_dim] * w1 + w2 * new[1:2]
        results.append(numer / (sums[0] * w0 + sums[1] * w1 + w2))
    for h in range(heads):
        rows = jnp.concatenate([x[h : h + 1] for x in results], axis=0)
        out_ref[:, h * head_dim : (h + 1) * head_dim] = rows.astype(jnp.bfloat16)


def finish(mine, theirs, queries, new_kv, heads):
    def kernel(*refs):
        finish_kernel(heads, *refs)

    seqs, _, head_dim = queries.shape
    return pl.pallas_call(
        kernel,
        out_shape=jax.ShapeDtypeStruct((seqs, heads * head_dim), jnp.bfloat16),
        compiler_params=LIMIT,
    )(mine, theirs, queries, new_kv)


def body(tokens, w_query, w_gate_up, key_cache, value_cache, new_kv, lengths):
    f32, bf16 = jnp.float32, jnp.bfloat16
    d, width, qw = tokens.shape[1], w_gate_up.shape[2], w_query.shape[1]
    seqs, _, head_dim = key_cache.shape

    keys_b, keys_c = beside(key_cache), other_core(key_cache)
    rows = spread(tokens, LATTICE, 32, far_groups()).reshape(64, d)
    rows, keys_b, keys_c = lax.optimization_barrier((rows, keys_b, keys_c))
    values_b = beside(value_cache)
    rows = spread(rows, PLANE, 4, near_groups()).reshape(256, d)
    rows, values_b = lax.optimization_barrier((rows, values_b))
    values_c, keys_d, values_d = other_core(value_cache), other_core(keys_b), other_core(values_b)

    got = exchange(project(rows, w_query.T, True), GX)
    got, values_c, keys_d = lax.optimization_barrier((got, values_c, keys_d))
    total = jnp.sum(got.astype(f32), axis=0)
    query = (total[:, :qw] + total[:, qw:]).astype(bf16)

    query = query.reshape(2, 2, 4, 2, qw).transpose(0, 2, 1, 3, 4).reshape(16, 2, qw)
    query = exchange(jnp.concatenate([query, query], axis=0), ALL, query_groups())
    gate_up = project(rows, w_gate_up.transpose(1, 2, 0).reshape(2 * width, d), False)
    query, gate_up, values_d = lax.optimization_barrier((query, gate_up, values_d))
    place = lax.axis_index(GX)
    block = lax.axis_index("xh") * 4 + lax.axis_index("z") // 2
    sender = jnp.where(place == block, place % 2, (place < block).astype(place.dtype))
    query = lax.dynamic_slice_in_dim(query, sender * 16, 16, 0)
    per_dev = 16 * qw // head_dim
    query = query.transpose(1, 0, 2).reshape(seqs, per_dev, head_dim)
    query = jnp.pad(query, ((0, 0), (0, 8 - per_dev), (0, 0)))
    gate_up, other = lax.optimization_barrier((gate_up, across(query)))
    queries = jnp.concatenate([query, other], axis=1)

    keys = (key_cache, keys_b, keys_c, keys_d)
    values = (value_cache, values_b, values_c, values_d)
    mine, theirs = attend(place, lengths, queries, keys, values, (0, 2, 1, 3))
    attended = finish(mine, across(theirs), queries, new_kv, per_dev)
    total = jnp.sum(exchange(gate_up, GX).astype(f32), axis=0)
    hidden = (jax.nn.silu(total[:, :width]) * total[:, width:]).astype(bf16)
    hidden = hidden.reshape(2, 2, 4, 2, width).transpose(0, 2, 1, 3, 4).reshape(32, width)
    return (hidden, attended)


def solution(mesh):
    fine = Mesh(mesh.devices.reshape(4, 2, 2, 8, 8), GX + GY)
    return jax.shard_map(
        body,
        mesh=fine,
        in_specs=(
            P(GY, GX),
            P(GX, GY),
            P(GX, None, GY),
            P(GY, GX, None),
            P(GY, GX, None),
            P(GY, None, None),
            P(GY),
        ),
        out_specs=(P(GX, GY), P(GY, GX)),
        check_vma=False,
    )
```
